32 devices in a mesh: seq: 16 (over z, y, x), fsdp: 2 (over core).
Axes of the slice: x: 2, y: 2, z: 4, core: 2. Of those that a mesh axis runs over, the one named last changes fastest.
Arguments:
- queries: bfloat16 [4096, 2048], P(('seq', 'fsdp')), may hold values from -4.5 to 4.5
- keys: bfloat16 [4096, 2048], P(('seq', 'fsdp')), may hold values from -4.5 to 4.5
- values: bfloat16 [4096, 2048], P(('seq', 'fsdp')), may hold values from -6 to 6
- grad_out: bfloat16 [4096, 2048], P(('seq', 'fsdp')), may hold values from -6 to 6
- out_proj: bfloat16 [2048, 2048], P(('seq', 'fsdp')), may hold values from -0.125 to 0.125
- lists: int32 [16, 8], replicated, may hold values from 0 to 14, as said below
- window: int32 [16], replicated, may hold values from 64 to 128
Outputs:
- layer_out: bfloat16 [4096, 2048], P(('seq', 'fsdp'))
- grad_queries: bfloat16 [4096, 2048], P(('seq', 'fsdp'))
- grad_keys: bfloat16 [4096, 2048], P(('seq', 'fsdp'))
- grad_values: bfloat16 [4096, 2048], P(('seq', 'fsdp'))
The draws below stay inside these ranges and needn't reach their ends.
Inputs may be any that keep to these rules, and one draw needn't show every extreme that they name: `lists`: within a row the ids are distinct; for b >= 1, row b holds the id b - 1.
All inputs are finite; a program needn't handle non-finite values.
Results may differ from the reference program's by a relative error of at most 0.025.
Values may be sent and summed in bfloat16 or wider, within the bound.
A program may use at most 128 MiB of HBM per device.

```python
import jax
import jax.numpy as jnp
from jax import lax

HEAD_COUNT = 16
HEAD_DIM = 128
OUT_DIM = 2048
TOK_DEV = 128
SUMMARY = 4
LISTED = 8
ATT_DIM = 2048
BLOCK_ROWS = 256
NBLOCKS = 16
SEQ_LEN = 4096
N_FSDP = 2


def draw_queries(key, part):
    result = jnp.clip(jax.random.normal(jax.random.fold_in(key, 712), (SEQ_LEN, ATT_DIM), jnp.float32), -4.5, 4.5)
    return result.astype(jnp.bfloat16)


def draw_keys(key, part):
    result = jnp.clip(jax.random.normal(jax.random.fold_in(key, 722), (SEQ_LEN, ATT_DIM), jnp.float32), -4.5, 4.5)
    return result.astype(jnp.bfloat16)


def draw_lists(key, part):
    block_ids = jnp.arange(NBLOCKS, dtype=jnp.int32)
    rows = block_ids[:, None]
    limit = jnp.maximum(rows, LISTED)
    noise = jax.random.randint(jax.random.fold_in(key, 731), (NBLOCKS, NBLOCKS), 0, 2 ** 16)
    score = noise * (2 * NBLOCKS) + block_ids[None, :]
    score = score + jnp.where(block_ids[None, :] >= limit, 2 ** 26, 0)
    score = jnp.where(block_ids[None, :] == rows - 1, -1, score)
    order = jnp.argsort(score, axis=1, stable=True)
    return order[:, :LISTED].astype(jnp.int32)


def draw_window(key, part):
    extent = jax.random.randint(jax.random.fold_in(key, 741), (NBLOCKS,), TOK_DEV // 2, TOK_DEV + 1)
    first = jax.random.randint(jax.random.fold_in(key, 742), (), 0, NBLOCKS)
    step = jax.random.randint(jax.random.fold_in(key, 743), (), 1, NBLOCKS)
    second = (first + step) % NBLOCKS
    extent = extent.at[first].set(TOK_DEV)
    extent = extent.at[second].set(TOK_DEV // 2)
    return extent.astype(jnp.int32)


def block_levels(rng, dims, shards, smallest, high):
    def one(axis_at, blocks):
        steps = jax.random.uniform(jax.random.fold_in(jax.random.fold_in(rng, 6), axis_at), (blocks,), jnp.float32, smallest / len(shards), high / len(shards))
        return jnp.repeat(jnp.exp(steps), dims[axis_at] // blocks).reshape((-1,) + (1,) * (len(dims) - axis_at - 1))

    gain = one(*shards[0])
    for cut in shards[1:]:
        gain = gain * one(*cut)
    return gain


def normal_values(stream_key, dims, scale, bound, split=(), kind=jnp.bfloat16):
    entries = jax.random.normal(stream_key, dims, jnp.float32) * scale
    if len(split) > 0:
        entries = block_levels(stream_key, dims, split, -0.22, 0.18) * entries
    return jnp.clip(entries, min=-bound, max=bound).astype(kind)


def setup_inputs(seed: int = 0) -> dict:
    key_list = jax.random.split(jax.random.key(seed), 8)
    return {
        "queries": draw_queries(jax.random.fold_in(key_list[7], 71), 0),
        "keys": draw_keys(jax.random.fold_in(key_list[7], 71), 0),
        "values": normal_values(key_list[2], (SEQ_LEN, ATT_DIM), 1.0, 6.0, ((0, 32),)),
        "grad_out": normal_values(key_list[3], (SEQ_LEN, OUT_DIM), 1.0, 6.0, ((0, 32),)),
        "out_proj": normal_values(key_list[4], (ATT_DIM, OUT_DIM), ATT_DIM ** -0.5, 0.125, ((0, 32),)),
        "lists": draw_lists(jax.random.fold_in(key_list[7], 71), 0),
        "window": draw_window(jax.random.fold_in(key_list[7], 71), 0),
    }


def reference(queries, keys, values, grad_out, out_proj, lists, window):
    f32 = jnp.float32
    ndev = NBLOCKS * N_FSDP
    nsum = NBLOCKS * SUMMARY
    scale = 1.0 / (HEAD_DIM ** 0.5)
    q_dev = queries.reshape(ndev, TOK_DEV, HEAD_COUNT, HEAD_DIM)
    k_dev = keys.reshape(ndev, TOK_DEV, HEAD_COUNT, HEAD_DIM)
    v_dev = values.reshape(ndev, TOK_DEV, HEAD_COUNT, HEAD_DIM)
    k_prev = jnp.concatenate([jnp.zeros_like(k_dev[:1]), k_dev[:-1]], axis=0)
    v_prev = jnp.concatenate([jnp.zeros_like(v_dev[:1]), v_dev[:-1]], axis=0)
    summ_k = keys.reshape(NBLOCKS, BLOCK_ROWS, ATT_DIM)[:, BLOCK_ROWS - SUMMARY:].reshape(nsum, HEAD_COUNT, HEAD_DIM).astype(f32)
    summ_v = values.reshape(NBLOCKS, BLOCK_ROWS, ATT_DIM)[:, BLOCK_ROWS - SUMMARY:].reshape(nsum, HEAD_COUNT, HEAD_DIM).astype(f32)
    block_ids = jnp.arange(NBLOCKS, dtype=jnp.int32)
    hits = jnp.any(lists[:, :, None] == block_ids[None, None, :], axis=1) & (block_ids[None, :] < block_ids[:, None])
    summ_valid = jnp.repeat(hits, SUMMARY, axis=1)
    rows_t = jnp.arange(TOK_DEV, dtype=jnp.int32)
    rows_u = jnp.arange(2 * TOK_DEV, dtype=jnp.int32)
    offset = rows_t[:, None] + TOK_DEV - rows_u[None, :]

    def gather_dev(dev):
        block = dev // N_FSDP
        q_here = q_dev[dev].astype(f32)
        key_all = jnp.concatenate([k_prev[dev].astype(f32), k_dev[dev].astype(f32), summ_k], axis=0)
        val_all = jnp.concatenate([v_prev[dev].astype(f32), v_dev[dev].astype(f32), summ_v], axis=0)
        loc_valid = (offset >= 0) & (offset < window[block]) & ((rows_u[None, :] >= TOK_DEV) | (dev > 0))
        valid = jnp.concatenate([loc_valid, jnp.broadcast_to(summ_valid[block][None, :], (TOK_DEV, nsum))], axis=1)
        score = jnp.einsum('thd,khd->htk', q_here, key_all) * scale
        masked = jnp.where(valid[None], score, -jnp.inf)
        top = jnp.max(masked, axis=-1, keepdims=True)
        expo = jnp.where(valid[None], jnp.exp(score - top), 0.0)
        prob = (expo / jnp.sum(expo, axis=-1, keepdims=True)).astype(jnp.bfloat16)
        return q_here, key_all, val_all, prob

    def forward_dev(dev):
        q_here, key_all, val_all, prob = gather_dev(dev)
        out = jnp.einsum('htk,khd->thd', prob.astype(f32), val_all)
        return out.reshape(TOK_DEV, ATT_DIM).astype(jnp.bfloat16)

    attn = lax.map(forward_dev, jnp.arange(ndev, dtype=jnp.int32)).reshape(SEQ_LEN, ATT_DIM)
    layer_out = jnp.dot(attn, out_proj, preferred_element_type=f32).astype(jnp.bfloat16)
    grad_attn = jnp.dot(grad_out, out_proj.T, preferred_element_type=f32).astype(jnp.bfloat16)
    grad_dev = grad_attn.reshape(ndev, TOK_DEV, HEAD_COUNT, HEAD_DIM)

    def backward_dev(carry, dev):
        q_here, key_all, val_all, prob = gather_dev(dev)
        prob32 = prob.astype(f32)
        grad_here = grad_dev[dev].astype(f32)
        grad_prob = jnp.einsum('thd,khd->htk', grad_here, val_all)
        delta = jnp.sum(prob32 * grad_prob, axis=-1, keepdims=True)
        grad_score = (prob32 * (grad_prob - delta) * scale).astype(jnp.bfloat16).astype(f32)
        grad_q = jnp.einsum('htk,khd->thd', grad_score, key_all).astype(jnp.bfloat16)
        grad_k = jnp.einsum('htk,thd->khd', grad_score, q_here)
        grad_v = jnp.einsum('htk,thd->khd', prob32, grad_here)
        carry = (carry[0] + grad_k[2 * TOK_DEV:], carry[1] + grad_v[2 * TOK_DEV:])
        return carry, (grad_q, grad_k[:2 * TOK_DEV], grad_v[:2 * TOK_DEV])

    start = (jnp.zeros((nsum, HEAD_COUNT, HEAD_DIM), f32), jnp.zeros((nsum, HEAD_COUNT, HEAD_DIM), f32))
    summ_grads, (grad_q, loc_k, loc_v) = lax.scan(backward_dev, start, jnp.arange(ndev, dtype=jnp.int32))
    pad_zero = jnp.zeros_like(loc_k[:1, :TOK_DEV])
    dev_k = loc_k[:, TOK_DEV:] + jnp.concatenate([loc_k[1:, :TOK_DEV], pad_zero], axis=0)
    dev_v = loc_v[:, TOK_DEV:] + jnp.concatenate([loc_v[1:, :TOK_DEV], pad_zero], axis=0)
    dev_k = dev_k.reshape(NBLOCKS, BLOCK_ROWS, ATT_DIM).at[:, BLOCK_ROWS - SUMMARY:].add(summ_grads[0].reshape(NBLOCKS, SUMMARY, ATT_DIM))
    dev_v = dev_v.reshape(NBLOCKS, BLOCK_ROWS, ATT_DIM).at[:, BLOCK_ROWS - SUMMARY:].add(summ_grads[1].reshape(NBLOCKS, SUMMARY, ATT_DIM))
    grad_queries = grad_q.reshape(SEQ_LEN, ATT_DIM)
    grad_keys = dev_k.reshape(SEQ_LEN, ATT_DIM).astype(jnp.bfloat16)
    grad_values = dev_v.reshape(SEQ_LEN, ATT_DIM).astype(jnp.bfloat16)
    return layer_out, grad_queries, grad_keys, grad_values
```

```python
import functools

import jax
import jax.numpy as jnp
from jax import lax
from jax.experimental import pallas as pl
from jax.experimental.pallas import tpu as pltpu
from jax.sharding import PartitionSpec as P

HEAD_DIM = 128
SUMMARY = 4
MESH = pl.DeviceIdType.MESH
ANY = pl.BlockSpec(memory_space=pl.ANY)


def place():
    block, member = lax.axis_index("seq"), lax.axis_index("fsdp")
    return block, member, block * lax.axis_size("fsdp") + member


def fetch_kernel(
    blocks, members, k_ref, v_ref, own_ref, pk_ref, pv_ref, sum_ref,
    send_sem, recv_sem, prev_send, prev_recv, loc_sem,
):
    block, member, dev = place()
    ndev = blocks * members
    last = member == members - 1

    def to_next(i, src, dst):
        after = lax.rem(dev + 1, ndev)
        return pltpu.make_async_remote_copy(
            src_ref=src, dst_ref=dst, send_sem=prev_send.at[i], recv_sem=prev_recv.at[i],
            device_id=(after // members, lax.rem(after, members)), device_id_type=MESH,
        )

    def summary_to(i):
        to = lax.rem(dev + 1 + i, ndev)
        return pltpu.make_async_remote_copy(
            src_ref=own_ref, dst_ref=sum_ref.at[block], send_sem=send_sem.at[i],
            recv_sem=recv_sem.at[block],
            device_id=(to // members, lax.rem(to, members)), device_id_type=MESH,
        )

    local = pltpu.make_async_copy(own_ref, sum_ref.at[block], loc_sem)

    @pl.when(last)
    def _():
        local.start()

        @pl.loop(0, ndev - 1)
        def _(i):
            summary_to(i).start()

    next_k, next_v = to_next(0, k_ref, pk_ref), to_next(1, v_ref, pv_ref)
    next_k.start()
    next_v.start()

    @pl.when(last)
    def _():
        local.wait()

        @pl.loop(0, ndev - 1)
        def _(i):
            summary_to(i).wait_send()

    @pl.loop(0, blocks)
    def _(j):
        @pl.when(jnp.logical_not(last & (j == block)))
        def _():
            pltpu.make_async_remote_copy(
                src_ref=own_ref, dst_ref=sum_ref.at[j], send_sem=send_sem.at[0],
                recv_sem=recv_sem.at[j], device_id=(block, member), device_id_type=MESH,
            ).wait_recv()

    next_k.wait()
    next_v.wait()


def fetch(keys, values, own, blocks, members):
    ndev = blocks * members
    return pl.pallas_call(
        functools.partial(fetch_kernel, blocks, members),
        out_shape=(
            jax.ShapeDtypeStruct(keys.shape, keys.dtype),
            jax.ShapeDtypeStruct(values.shape, values.dtype),
            jax.ShapeDtypeStruct((blocks,) + own.shape, own.dtype),
        ),
        in_specs=[ANY] * 3,
        out_specs=(ANY,) * 3,
        scratch_shapes=[
            pltpu.SemaphoreType.DMA((ndev,)),
            pltpu.SemaphoreType.DMA((blocks,)),
            pltpu.SemaphoreType.DMA((2,)),
            pltpu.SemaphoreType.DMA((2,)),
            pltpu.SemaphoreType.DMA,
        ],
        compiler_params=pltpu.CompilerParams(has_side_effects=True),
        name="fetch",
    )(keys, values, own)


def give_back_kernel(
    blocks, members, ret_ref, gsum_ref, got_ref, parts_ref,
    send_sem, recv_sem, ret_send, ret_recv,
):
    block, member, dev = place()
    ndev = blocks * members
    before = lax.rem(dev + ndev - 1, ndev)
    back = pltpu.make_async_remote_copy(
        src_ref=ret_ref, dst_ref=got_ref, send_sem=ret_send, recv_sem=ret_recv,
        device_id=(before // members, lax.rem(before, members)), device_id_type=MESH,
    )

    def part_to(m):
        return pltpu.make_async_remote_copy(
            src_ref=gsum_ref.at[m], dst_ref=parts_ref.at[dev], send_sem=send_sem.at[m],
            recv_sem=recv_sem.at[dev], device_id=(m, members - 1), device_id_type=MESH,
        )

    @pl.loop(0, blocks)
    def _(m):
        @pl.when(m < block)
        def _():
            part_to(m).start()

    back.start()

    @pl.loop(0, blocks)
    def _(m):
        @pl.when(m < block)
        def _():
            part_to(m).wait_send()

    @pl.when(member == members - 1)
    def _():
        @pl.loop(0, ndev)
        def _(j):
            @pl.when(j >= (block + 1) * members)
            def _():
                pltpu.make_async_remote_copy(
                    src_ref=gsum_ref.at[0], dst_ref=parts_ref.at[j], send_sem=send_sem.at[0],
                    recv_sem=recv_sem.at[j], device_id=(block, member), device_id_type=MESH,
                ).wait_recv()

    back.wait()


def give_back(ret, gsum, blocks, members):
    ndev = blocks * members
    return pl.pallas_call(
        functools.partial(give_back_kernel, blocks, members),
        out_shape=(
            jax.ShapeDtypeStruct(ret.shape, ret.dtype),
            jax.ShapeDtypeStruct((ndev,) + gsum.shape[1:], gsum.dtype),
        ),
        in_specs=[ANY] * 2,
        out_specs=(ANY,) * 2,
        scratch_shapes=[
            pltpu.SemaphoreType.DMA((blocks,)),
            pltpu.SemaphoreType.DMA((ndev,)),
            pltpu.SemaphoreType.DMA,
            pltpu.SemaphoreType.DMA,
        ],
        compiler_params=pltpu.CompilerParams(has_side_effects=True),
        name="give_back",
    )(ret, gsum)


def dot(a, b, da, db):
    return lax.dot_general(a, b, (((da,), (db,)), ((), ())), preferred_element_type=jnp.float32)


def attend_kernel(
    q_ref, k_ref, v_ref, pk_ref, pv_ref, ks_ref, vs_ref, go_ref, w_ref, valid_ref,
    out_ref, gq_ref, gk_ref, gv_ref, ret_ref, gs_ref, total,
):
    f32, b16 = jnp.float32, jnp.bfloat16
    tokens = q_ref.shape[0]
    scale = 1.0 / HEAD_DIM**0.5
    h = pl.program_id(0)
    q, w = q_ref[...], w_ref[...]
    key = jnp.concatenate([pk_ref[...], k_ref[...], ks_ref[...]], axis=0)
    val = jnp.concatenate([pv_ref[...], v_ref[...], vs_ref[...]], axis=0)
    valid = valid_ref[...] > 0
    grad = dot(go_ref[...], w, 1, 1).astype(b16)
    score = jnp.where(valid, dot(q, key, 1, 1) * scale, -jnp.inf)
    top = jnp.max(score, axis=-1, keepdims=True)
    expo = jnp.exp(score - top)
    prob = (expo / jnp.sum(expo, axis=-1, keepdims=True)).astype(b16)
    attn = dot(prob, val, 1, 0).astype(b16)
    part = dot(attn, w, 1, 0)

    @pl.when(h == 0)
    def _():
        total[...] = part

    @pl.when(h > 0)
    def _():
        total[...] += part

    prob32 = prob.astype(f32)
    gprob = dot(grad, val, 1, 1)
    delta = jnp.sum(prob32 * gprob, axis=-1, keepdims=True)
    gscore = (prob32 * (gprob - delta) * scale).astype(b16)
    gq_ref[...] = dot(gscore, key, 1, 0).astype(b16)
    gk = dot(gscore, q, 0, 0)
    gv = dot(prob, grad, 0, 0)
    ret_ref[0] = gk[:tokens].astype(b16)
    ret_ref[1] = gv[:tokens].astype(b16)
    gk_ref[...] = gk[tokens : 2 * tokens]
    gv_ref[...] = gv[tokens : 2 * tokens]
    gs_ref[0] = gk[2 * tokens :].astype(b16)
    gs_ref[1] = gv[2 * tokens :].astype(b16)

    @pl.when(h == pl.num_programs(0) - 1)
    def _():
        out_ref[...] = total[...].astype(b16)


def attend(q, k, v, pk, pv, ks, vs, go, w, valid):
    tokens, width = q.shape
    nsum, wide = ks.shape[0], go.shape[1]
    f32, b16 = jnp.float32, jnp.bfloat16
    col = pl.BlockSpec((tokens, HEAD_DIM), lambda h: (0, h))
    scol = pl.BlockSpec((nsum, HEAD_DIM), lambda h: (0, h))
    whole = pl.BlockSpec((tokens, wide), lambda h: (0, 0))
    return pl.pallas_call(
        attend_kernel,
        grid=(width // HEAD_DIM,),
        in_specs=[
            col, col, col, col, col, scol, scol, whole,
            pl.BlockSpec((HEAD_DIM, wide), lambda h: (h, 0)),
            pl.BlockSpec(valid.shape, lambda h: (0, 0)),
        ],
        out_specs=(
            whole, col, col, col,
            pl.BlockSpec((2, tokens, HEAD_DIM), lambda h: (0, 0, h)),
            pl.BlockSpec((2, nsum, HEAD_DIM), lambda h: (0, 0, h)),
        ),
        out_shape=(
            jax.ShapeDtypeStruct((tokens, wide), b16),
            jax.ShapeDtypeStruct((tokens, width), b16),
            jax.ShapeDtypeStruct((tokens, width), f32),
            jax.ShapeDtypeStruct((tokens, width), f32),
            jax.ShapeDtypeStruct((2, tokens, width), b16),
            jax.ShapeDtypeStruct((2, nsum, width), b16),
        ),
        scratch_shapes=[pltpu.VMEM((tokens, wide), f32)],
        compiler_params=pltpu.CompilerParams(vmem_limit_bytes=32 * 2**20),
        name="attend",
    )(q, k, v, pk, pv, ks, vs, go, w, valid)


def local(queries, keys, values, grad_out, out_proj, lists, window):
    f32 = jnp.float32
    tokens, width = queries.shape
    blocks, members = lax.axis_size("seq"), lax.axis_size("fsdp")
    ndev = blocks * members
    block, member, dev = place()
    nsum = blocks * SUMMARY
    whole = lax.all_gather(out_proj, ("seq", "fsdp"), axis=0, tiled=True)
    own = jnp.stack([keys[tokens - SUMMARY :], values[tokens - SUMMARY :]])
    own = own.reshape(16, 2 * SUMMARY * width // 16)
    pk, pv, sums = fetch(keys, values, own, blocks, members)
    sums = sums.reshape(blocks, 2, SUMMARY, width)
    ks = sums[:, 0].reshape(nsum, width)
    vs = sums[:, 1].reshape(nsum, width)

    my_list = lax.dynamic_index_in_dim(lists, block, 0, keepdims=False)
    ids = jnp.arange(nsum, dtype=jnp.int32) // SUMMARY
    hit = jnp.any(my_list[:, None] == ids[None, :], axis=0) & (ids < block)
    extent = lax.dynamic_index_in_dim(window, block, 0, keepdims=False)
    rows = jnp.arange(tokens, dtype=jnp.int32)
    cols = jnp.arange(2 * tokens, dtype=jnp.int32)
    offset = rows[:, None] + tokens - cols[None, :]
    near = (offset >= 0) & (offset < extent) & ((cols[None, :] >= tokens) | (dev > 0))
    valid = jnp.concatenate([near, jnp.broadcast_to(hit[None], (tokens, nsum))], axis=1)

    out, gq, gk, gv, ret, gs = attend(
        queries, keys, values, pk, pv, ks, vs, grad_out, whole, valid.astype(f32)
    )
    gs = gs.reshape(2, blocks, SUMMARY, width).transpose(1, 0, 2, 3)
    got, parts = give_back(ret, gs.reshape(blocks, 16, -1), blocks, members)
    got = jnp.where(dev < ndev - 1, got.astype(f32), 0.0)
    sent = (jnp.arange(ndev) >= (block + 1) * members) & (member == members - 1)
    extra = jnp.sum(jnp.where(sent[:, None, None], parts.astype(f32), 0.0), axis=0)
    extra = extra.reshape(2, SUMMARY, width)
    pad = jnp.pad(extra, ((0, 0), (tokens - SUMMARY, 0), (0, 0)))
    grad_keys = (gk + got[0] + pad[0]).astype(jnp.bfloat16)
    grad_values = (gv + got[1] + pad[1]).astype(jnp.bfloat16)
    return out, gq, grad_keys, grad_values


def solution(mesh):
    split = P(("seq", "fsdp"), None)
    return jax.shard_map(
        local, mesh=mesh, in_specs=(split,) * 5 + (P(), P()), out_specs=(split,) * 4, check_vma=False
    )
```

```python
import functools

import jax
import jax.numpy as jnp
from jax import lax
from jax.experimental import pallas as pl
from jax.experimental.pallas import tpu as pltpu
from jax.sharding import PartitionSpec as P

HEAD_DIM = 128
HEADS = 4
CUTS = 2
SUMMARY = 4
MESH = pl.DeviceIdType.MESH
ANY = pl.BlockSpec(memory_space=pl.ANY)


def place():
    block, member = lax.axis_index("seq"), lax.axis_index("fsdp")
    return block, member, block * lax.axis_size("fsdp") + member


def ring_block(p, blocks):
    if blocks != 16:
        return p
    col, up = p // 4, lax.rem(p, 4)
    z = up + lax.rem(col, 2) * (3 - 2 * up)
    return z * 4 + (col // 2) * 2 + lax.rem((col + 1) // 2, 2)


def ring_place(block, blocks):
    if blocks != 16:
        return block
    z, y, x = block // 4, lax.rem(block // 2, 2), lax.rem(block, 2)
    col = 2 * y + lax.rem(x + y, 2)
    return col * 4 + z + lax.rem(col, 2) * (3 - 2 * z)


class Ring:
    def __init__(self, blocks, w_ref, all_ref, sems):
        self.block, self.member, self.dev = place()
        self.blocks, self.w_ref, self.all_ref = blocks, w_ref, all_ref
        self.f_send, self.f_recv, self.b_send, self.b_recv, self.s_send, self.s_recv, self.l_sem = sems
        self.rows = w_ref.shape[0] // CUTS
        self.me = ring_place(self.block, blocks)
        self.f_count = blocks // 2 * CUTS
        self.b_count = (blocks - 1 - blocks // 2) * CUTS

    def chunk(self, block, member, c):
        return self.all_ref.at[block * 2 + member, pl.ds(pl.multiple_of(c * self.rows, self.rows), self.rows)]

    def copy(self, i, back, sends, recvs):
        n, k = self.blocks, i // CUTS
        shard = ring_block(lax.rem(self.me + n + (k if back else -k), n), n)
        to = ring_block(lax.rem(self.me + n + (-1 if back else 1), n), n)
        ref = self.chunk(shard, self.member, lax.rem(i, CUTS))
        return pltpu.make_async_remote_copy(
            src_ref=ref, dst_ref=ref, send_sem=sends.at[i], recv_sem=recvs.at[i],
            device_id=(to, self.member), device_id_type=MESH,
        )

    def forward(self, i):
        return self.copy(i, False, self.f_send, self.f_recv)

    def backward(self, i):
        return self.copy(i, True, self.b_send, self.b_recv)

    def aside(self, block, c):
        ref = self.chunk(block, self.member, c)
        at = block * CUTS + c
        return pltpu.make_async_remote_copy(
            src_ref=ref, dst_ref=ref, send_sem=self.s_send.at[at], recv_sem=self.s_recv.at[at],
            device_id=(self.block, 1 - self.member), device_id_type=MESH,
        )

    def arrived(self, j, back):
        n, k = self.blocks, j // CUTS
        shard = ring_block(lax.rem(self.me + n + (k + 1 if back else -k - 1), n), n)
        c = lax.rem(j, CUTS)
        ref = self.chunk(shard, self.member, c)
        pltpu.make_async_remote_copy(
            src_ref=ref, dst_ref=ref, send_sem=self.f_send.at[0],
            recv_sem=(self.b_recv if back else self.f_recv).at[j],
            device_id=(self.block, 1 - self.member), device_id_type=MESH,
        ).wait_recv()
        return shard, c

    def run(self):
        mine = pltpu.make_async_copy(self.w_ref, self.all_ref.at[self.dev], self.l_sem)
        mine.start()
        mine.wait()
        for i in range(CUTS):
            self.forward(i).start()
            self.backward(i).start()
        for c in range(CUTS):
            self.aside(self.block, c).start()

        @pl.loop(0, self.f_count)
        def _(j):
            shard, c = self.arrived(j, False)

            @pl.when(j + CUTS < self.f_count)
            def _():
                self.forward(j + CUTS).start()

            self.aside(shard, c).start()

            @pl.when(j < self.b_count)
            def _():
                shard, c = self.arrived(j, True)

                @pl.when(j + CUTS < self.b_count)
                def _():
                    self.backward(j + CUTS).start()

                self.aside(shard, c).start()

        @pl.loop(0, self.f_count)
        def _(i):
            self.forward(i).wait_send()

        @pl.loop(0, self.b_count)
        def _(i):
            self.backward(i).wait_send()

        @pl.loop(0, self.blocks * CUTS)
        def _(a):
            block, c = a // CUTS, lax.rem(a, CUTS)
            self.aside(block, c).wait_send()
            ref = self.chunk(block, 1 - self.member, c)
            pltpu.make_async_remote_copy(
                src_ref=ref, dst_ref=ref, send_sem=self.s_send.at[a], recv_sem=self.s_recv.at[a],
                device_id=(self.block, 1 - self.member), device_id_type=MESH,
            ).wait_recv()


def fetch_kernel(blocks, members, ring, *refs):
    if ring:
        w_ref, refs = refs[0], refs[1:]
        k_ref, v_ref, own_ref, all_ref = refs[:4]
        refs = refs[4:]
    else:
        k_ref, v_ref, own_ref = refs[:3]
        refs = refs[3:]
    pk_ref, pv_ref, sum_ref, send_sem, recv_sem, prev_send, prev_recv, loc_sem = refs[:8]
    block, member, dev = place()
    ndev = blocks * members
    last = member == members - 1

    def to_next(i, src, dst):
        after = lax.rem(dev + 1, ndev)
        return pltpu.make_async_remote_copy(
            src_ref=src, dst_ref=dst, send_sem=prev_send.at[i], recv_sem=prev_recv.at[i],
            device_id=(after // members, lax.rem(after, members)), device_id_type=MESH,
        )

    def summary_to(i):
        to = lax.rem(dev + 1 + i, ndev)
        return pltpu.make_async_remote_copy(
            src_ref=own_ref, dst_ref=sum_ref.at[block], send_sem=send_sem.at[i],
            recv_sem=recv_sem.at[block],
            device_id=(to // members, lax.rem(to, members)), device_id_type=MESH,
        )

    local = pltpu.make_async_copy(own_ref, sum_ref.at[block], loc_sem)

    @pl.when(last)
    def _():
        local.start()

        @pl.loop(0, ndev - 1)
        def _(i):
            summary_to(i).start()

    next_k, next_v = to_next(0, k_ref, pk_ref), to_next(1, v_ref, pv_ref)
    next_k.start()
    next_v.start()
    if ring:
        Ring(blocks, w_ref, all_ref, refs[8:]).run()

    @pl.when(last)
    def _():
        local.wait()

        @pl.loop(0, ndev - 1)
        def _(i):
            summary_to(i).wait_send()

    @pl.loop(0, blocks)
    def _(j):
        @pl.when(jnp.logical_not(last & (j == block)))
        def _():
            pltpu.make_async_remote_copy(
                src_ref=own_ref, dst_ref=sum_ref.at[j], send_sem=send_sem.at[0],
                recv_sem=recv_sem.at[j], device_id=(block, member), device_id_type=MESH,
            ).wait_recv()

    next_k.wait()
    next_v.wait()


def fetch(w, keys, values, own, blocks, members):
    ndev = blocks * members
    dma = pltpu.SemaphoreType.DMA
    ring = members == 2 and blocks > 2 and w.shape[0] % (16 * CUTS) == 0
    outs = (
        jax.ShapeDtypeStruct(keys.shape, keys.dtype),
        jax.ShapeDtypeStruct(values.shape, values.dtype),
        jax.ShapeDtypeStruct((blocks,) + own.shape, own.dtype),
    )
    args = (keys, values, own)
    sems = [dma((ndev,)), dma((blocks,)), dma((2,)), dma((2,)), dma]
    if ring:
        outs = (jax.ShapeDtypeStruct((ndev,) + w.shape, w.dtype),) + outs
        args = (w,) + args
        steps = blocks * CUTS
        sems += [dma((steps,))] * 6 + [dma]
    got = pl.pallas_call(
        functools.partial(fetch_kernel, blocks, members, ring),
        out_shape=outs,
        in_specs=[ANY] * len(args),
        out_specs=(ANY,) * len(outs),
        scratch_shapes=sems,
        compiler_params=pltpu.CompilerParams(has_side_effects=True),
        name="fetch",
    )(*args)
    if ring:
        return (got[0].reshape(ndev * w.shape[0], w.shape[1]),) + tuple(got[1:])
    return (lax.all_gather(w, ("seq", "fsdp"), axis=0, tiled=True),) + tuple(got)


def give_back_kernel(
    blocks, members, ret_ref, gsum_ref, got_ref, parts_ref,
    send_sem, recv_sem, ret_send, ret_recv,
):
    block, member, dev = place()
    ndev = blocks * members
    before = lax.rem(dev + ndev - 1, ndev)
    back = pltpu.make_async_remote_copy(
        src_ref=ret_ref, dst_ref=got_ref, send_sem=ret_send, recv_sem=ret_recv,
        device_id=(before // members, lax.rem(before, members)), device_id_type=MESH,
    )

    def part_to(m):
        return pltpu.make_async_remote_copy(
            src_ref=gsum_ref.at[m], dst_ref=parts_ref.at[dev], send_sem=send_sem.at[m],
            recv_sem=recv_sem.at[dev], device_id=(m, members - 1), device_id_type=MESH,
        )

    back.start()

    @pl.loop(0, blocks)
    def _(m):
        @pl.when(m < block)
        def _():
            part_to(m).start()

    @pl.loop(0, blocks)
    def _(m):
        @pl.when(m < block)
        def _():
            part_to(m).wait_send()

    @pl.when(member == members - 1)
    def _():
        @pl.loop(0, ndev)
        def _(j):
            @pl.when(j >= (block + 1) * members)
            def _():
                pltpu.make_async_remote_copy(
                    src_ref=gsum_ref.at[0], dst_ref=parts_ref.at[j], send_sem=send_sem.at[0],
                    recv_sem=recv_sem.at[j], device_id=(block, member), device_id_type=MESH,
                ).wait_recv()

    back.wait()


def give_back(ret, gsum, blocks, members):
    ndev = blocks * members
    return pl.pallas_call(
        functools.partial(give_back_kernel, blocks, members),
        out_shape=(
            jax.ShapeDtypeStruct(ret.shape, ret.dtype),
            jax.ShapeDtypeStruct((ndev,) + gsum.shape[1:], gsum.dtype),
        ),
        in_specs=[ANY] * 2,
        out_specs=(ANY,) * 2,
        scratch_shapes=[
            pltpu.SemaphoreType.DMA((blocks,)),
            pltpu.SemaphoreType.DMA((ndev,)),
            pltpu.SemaphoreType.DMA,
            pltpu.SemaphoreType.DMA,
        ],
        compiler_params=pltpu.CompilerParams(has_side_effects=True),
        name="give_back",
    )(ret, gsum)


def dot(a, b, da, db):
    return lax.dot_general(a, b, (((da,), (db,)), ((), ())), preferred_element_type=jnp.float32)


def attend_kernel(
    q_ref, k_ref, v_ref, pk_ref, pv_ref, ks_ref, vs_ref, go_ref, w_ref, valid_ref,
    out_ref, gq_ref, gk_ref, gv_ref, ret_ref, gs_ref, total,
):
    f32, b16 = jnp.float32, jnp.bfloat16
    tokens = q_ref.shape[0]
    scale = 1.0 / HEAD_DIM**0.5
    h = pl.program_id(0)
    w = w_ref[...]
    valid = valid_ref[...] > 0
    grads = dot(go_ref[...], w, 1, 1).astype(b16)
    attns = []
    for i in range(HEADS):
        at = slice(i * HEAD_DIM, (i + 1) * HEAD_DIM)
        q, grad = q_ref[:, at], grads[:, at]
        key = jnp.concatenate([pk_ref[:, at], k_ref[:, at], ks_ref[:, at]], axis=0)
        val = jnp.concatenate([pv_ref[:, at], v_ref[:, at], vs_ref[:, at]], axis=0)
        score = jnp.where(valid, dot(q, key, 1, 1) * scale, -jnp.inf)
        top = jnp.max(score, axis=-1, keepdims=True)
        expo = jnp.exp(score - top)
        prob = (expo / jnp.sum(expo, axis=-1, keepdims=True)).astype(b16)
        attns.append(dot(prob, val, 1, 0).astype(b16))
        prob32 = prob.astype(f32)
        gprob = dot(grad, val, 1, 1)
        delta = jnp.sum(prob32 * gprob, axis=-1, keepdims=True)
        gscore = (prob32 * (gprob - delta) * scale).astype(b16)
        gq_ref[:, at] = dot(gscore, key, 1, 0).astype(b16)
        gk = dot(gscore, q, 0, 0)
        gv = dot(prob, grad, 0, 0)
        ret_ref[0, :, at] = gk[:tokens].astype(b16)
        ret_ref[1, :, at] = gv[:tokens].astype(b16)
        gk_ref[:, at] = gk[tokens : 2 * tokens]
        gv_ref[:, at] = gv[tokens : 2 * tokens]
        gs_ref[0, :, at] = gk[2 * tokens :].astype(b16)
        gs_ref[1, :, at] = gv[2 * tokens :].astype(b16)
    part = dot(jnp.concatenate(attns, axis=1), w, 1, 0)

    @pl.when(h == 0)
    def _():
        total[...] = part

    @pl.when(h > 0)
    def _():
        total[...] += part

    @pl.when(h == pl.num_programs(0) - 1)
    def _():
        out_ref[...] = total[...].astype(b16)


def attend(q, k, v, pk, pv, ks, vs, go, w, valid):
    tokens, width = q.shape
    nsum, wide = ks.shape[0], go.shape[1]
    f32, b16 = jnp.float32, jnp.bfloat16
    step = HEADS * HEAD_DIM
    col = pl.BlockSpec((tokens, step), lambda h: (0, h))
    scol = pl.BlockSpec((nsum, step), lambda h: (0, h))
    whole = pl.BlockSpec((tokens, wide), lambda h: (0, 0))
    return pl.pallas_call(
        attend_kernel,
        grid=(width // step,),
        in_specs=[
            col, col, col, col, col, scol, scol, whole,
            pl.BlockSpec((step, wide), lambda h: (h, 0)),
            pl.BlockSpec(valid.shape, lambda h: (0, 0)),
        ],
        out_specs=(
            whole, col, col, col,
            pl.BlockSpec((2, tokens, step), lambda h: (0, 0, h)),
            pl.BlockSpec((2, nsum, step), lambda h: (0, 0, h)),
        ),
        out_shape=(
            jax.ShapeDtypeStruct((tokens, wide), b16),
            jax.ShapeDtypeStruct((tokens, width), b16),
            jax.ShapeDtypeStruct((tokens, width), f32),
            jax.ShapeDtypeStruct((tokens, width), f32),
            jax.ShapeDtypeStruct((2, tokens, width), b16),
            jax.ShapeDtypeStruct((2, nsum, width), b16),
        ),
        scratch_shapes=[pltpu.VMEM((tokens, wide), f32)],
        compiler_params=pltpu.CompilerParams(vmem_limit_bytes=56 * 2**20),
        name="attend",
    )(q, k, v, pk, pv, ks, vs, go, w, valid)


def local(queries, keys, values, grad_out, out_proj, lists, window):
    f32 = jnp.float32
    tokens, width = queries.shape
    blocks, members = lax.axis_size("seq"), lax.axis_size("fsdp")
    ndev = blocks * members
    block, member, dev = place()
    nsum = blocks * SUMMARY
    own = jnp.stack([keys[tokens - SUMMARY :], values[tokens - SUMMARY :]])
    own = own.reshape(16, 2 * SUMMARY * width // 16)
    whole, pk, pv, sums = fetch(out_proj, keys, values, own, blocks, members)
    sums = sums.reshape(blocks, 2, SUMMARY, width)
    ks = sums[:, 0].reshape(nsum, width)
    vs = sums[:, 1].reshape(nsum, width)

    my_list = lax.dynamic_index_in_dim(lists, block, 0, keepdims=False)
    ids = jnp.arange(nsum, dtype=jnp.int32) // SUMMARY
    hit = jnp.any(my_list[:, None] == ids[None, :], axis=0) & (ids < block)
    extent = lax.dynamic_index_in_dim(window, block, 0, keepdims=False)
    rows = jnp.arange(tokens, dtype=jnp.int32)
    cols = jnp.arange(2 * tokens, dtype=jnp.int32)
    offset = rows[:, None] + tokens - cols[None, :]
    near = (offset >= 0) & (offset < extent) & ((cols[None, :] >= tokens) | (dev > 0))
    valid = jnp.concatenate([near, jnp.broadcast_to(hit[None], (tokens, nsum))], axis=1)

    out, gq, gk, gv, ret, gs = attend(
        queries, keys, values, pk, pv, ks, vs, grad_out, whole, valid.astype(f32)
    )
    gs = gs.reshape(2, blocks, SUMMARY, width).transpose(1, 0, 2, 3)
    got, parts = give_back(ret, gs.reshape(blocks, 16, -1), blocks, members)
    got = jnp.where(dev < ndev - 1, got.astype(f32), 0.0)
    sent = (jnp.arange(ndev) >= (block + 1) * members) & (member == members - 1)
    extra = jnp.sum(jnp.where(sent[:, None, None], parts.astype(f32), 0.0), axis=0)
    extra = extra.reshape(2, SUMMARY, width)
    pad = jnp.pad(extra, ((0, 0), (tokens - SUMMARY, 0), (0, 0)))
    grad_keys = (gk + got[0] + pad[0]).astype(jnp.bfloat16)
    grad_values = (gv + got[1] + pad[1]).astype(jnp.bfloat16)
    return out, gq, grad_keys, grad_values


def solution(mesh):
    split = P(("seq", "fsdp"), None)
    return jax.shard_map(
        local, mesh=mesh, in_specs=(split,) * 5 + (P(), P()), out_specs=(split,) * 4, check_vma=False
    )
```

```python
import functools

import jax
import jax.numpy as jnp
from jax import lax
from jax.experimental import pallas as pl
from jax.experimental.pallas import tpu as pltpu
from jax.sharding import PartitionSpec as P

HEAD_DIM = 128
HEADS = 4
SUMMARY = 4
MESH = pl.DeviceIdType.MESH
ANY = pl.BlockSpec(memory_space=pl.ANY)


def place():
    block, member = lax.axis_index("seq"), lax.axis_index("fsdp")
    return block, member, block * lax.axis_size("fsdp") + member


class Grid:
    def __init__(self, w_ref, all_ref, sems):
        self.block, self.member, self.dev = place()
        self.z, self.y, self.x = self.block // 4, lax.rem(self.block // 2, 2), lax.rem(self.block, 2)
        self.w_ref, self.all_ref, self.rows = w_ref, all_ref, w_ref.shape[0] // 2
        (self.z_send, self.z_recv, self.x_send, self.x_recv, self.y_send, self.y_recv, self.dx_send,
         self.dx_recv, self.dy_send, self.dy_recv, self.s_send, self.s_recv, self.l_sem) = sems

    def at(self, z, dy=0, dx=0):
        y = 1 - self.y if dy else self.y
        x = 1 - self.x if dx else self.x
        return z * 4 + y * 2 + x

    def ref(self, block, half=None, other=False):
        shard = block * 2 + (1 - self.member if other else self.member)
        if half is None:
            return self.all_ref.at[shard]
        return self.all_ref.at[shard, pl.ds(half * self.rows, self.rows)]

    def copy(self, ref, to, send, recv):
        return pltpu.make_async_remote_copy(
            src_ref=ref, dst_ref=ref, send_sem=send, recv_sem=recv,
            device_id=(to, self.member), device_id_type=MESH,
        )

    def arrived(self, ref, recv):
        self.copy(ref, self.at(self.z, dx=1), self.x_send.at[0], recv).wait_recv()

    def aside(self, block, half=None, other=False):
        ref = self.ref(block, half, other)
        i = block * 2 + (half or 0)
        return pltpu.make_async_remote_copy(
            src_ref=ref, dst_ref=ref, send_sem=self.s_send.at[i], recv_sem=self.s_recv.at[i],
            device_id=(self.block, 1 - self.member), device_id_type=MESH,
        )

    def up(self, z):
        return self.copy(self.ref(self.at(z)), self.at(self.z + 1), self.z_send.at[z], self.z_recv.at[z])

    def down(self, z):
        return self.copy(self.ref(self.at(z)), self.at(self.z - 1), self.z_send.at[4 + z], self.z_recv.at[z])

    def to_x(self, z):
        return self.copy(self.ref(self.at(z)), self.at(self.z, dx=1), self.x_send.at[z], self.x_recv.at[z])

    def to_y(self, z):
        return self.copy(self.ref(self.at(z)), self.at(self.z, dy=1), self.y_send.at[z], self.y_recv.at[z])

    def on_y(self, z):
        return self.copy(self.ref(self.at(z, dx=1), 0), self.at(self.z, dy=1), self.dy_send.at[z], self.dy_recv.at[z])

    def on_x(self, z):
        return self.copy(self.ref(self.at(z, dy=1), 1), self.at(self.z, dx=1), self.dx_send.at[z], self.dx_recv.at[z])

    def spread(self, z, step):
        if step:
            self.arrived(self.ref(self.at(z)), self.z_recv.at[z])
        if step >= 0:
            @pl.when(self.z > 0)
            def _():
                self.down(z).start()
        if step <= 0:
            @pl.when(self.z < 3)
            def _():
                self.up(z).start()
        self.to_x(z).start()
        self.to_y(z).start()
        self.aside(self.at(z)).start()

    def turn(self, z):
        self.arrived(self.ref(self.at(z, dx=1)), self.x_recv.at[z])
        self.on_y(z).start()
        self.aside(self.at(z, dx=1)).start()
        self.arrived(self.ref(self.at(z, dy=1)), self.y_recv.at[z])
        self.on_x(z).start()
        self.aside(self.at(z, dy=1)).start()

    def corner(self, z):
        self.arrived(self.ref(self.at(z, 1, 1), 0), self.dy_recv.at[z])
        self.aside(self.at(z, 1, 1), 0).start()
        self.arrived(self.ref(self.at(z, 1, 1), 1), self.dx_recv.at[z])
        self.aside(self.at(z, 1, 1), 1).start()

    def each(self, step, do):
        z = self.z + step

        @pl.when((z >= 0) & (z < 4))
        def _():
            do(z)

    def run(self):
        mine = pltpu.make_async_copy(self.w_ref, self.all_ref.at[self.dev], self.l_sem)
        mine.start()
        mine.wait()
        for far in range(4):
            steps = (far, -far) if far else (0,)
            for step in steps:
                self.each(step, functools.partial(self.spread, step=step))
            for step in steps:
                self.each(step, self.turn)
        for far in range(4):
            for step in (far, -far) if far else (0,):
                self.each(step, self.corner)

        @pl.loop(0, 4)
        def _(z):
            @pl.when((z >= self.z) & (self.z > 0))
            def _():
                self.down(z).wait_send()

            @pl.when((z <= self.z) & (self.z < 3))
            def _():
                self.up(z).wait_send()

            for move in (self.to_x, self.to_y, self.on_x, self.on_y):
                move(z).wait_send()
            for dy, dx, half in ((0, 0, None), (0, 1, None), (1, 0, None), (1, 1, 0), (1, 1, 1)):
                self.aside(self.at(z, dy, dx), half).wait_send()
                self.aside(self.at(z, dy, dx), half, True).wait_recv()


def fetch_kernel(blocks, members, grid, *refs):
    if grid:
        w_ref, refs = refs[0], refs[1:]
        k_ref, v_ref, own_ref, all_ref = refs[:4]
        refs = refs[4:]
    else:
        k_ref, v_ref, own_ref = refs[:3]
        refs = refs[3:]
    pk_ref, pv_ref, sum_ref, send_sem, recv_sem, prev_send, prev_recv, loc_sem = refs[:8]
    block, member, dev = place()
    ndev = blocks * members
    last = member == members - 1

    def to_next(i, src, dst):
        after = lax.rem(dev + 1, ndev)
        return pltpu.make_async_remote_copy(
            src_ref=src, dst_ref=dst, send_sem=prev_send.at[i], recv_sem=prev_recv.at[i],
            device_id=(after // members, lax.rem(after, members)), device_id_type=MESH,
        )

    def summary_to(i):
        to = lax.rem(dev + 1 + i, ndev)
        return pltpu.make_async_remote_copy(
            src_ref=own_ref, dst_ref=sum_ref.at[block], send_sem=send_sem.at[i],
            recv_sem=recv_sem.at[block],
            device_id=(to // members, lax.rem(to, members)), device_id_type=MESH,
        )

    local = pltpu.make_async_copy(own_ref, sum_ref.at[block], loc_sem)

    @pl.when(last)
    def _():
        local.start()

        @pl.loop(0, ndev - 1)
        def _(i):
            summary_to(i).start()

    next_k, next_v = to_next(0, k_ref, pk_ref), to_next(1, v_ref, pv_ref)
    next_k.start()
    next_v.start()
    if grid:
        Grid(w_ref, all_ref, refs[8:]).run()

    @pl.when(last)
    def _():
        local.wait()

        @pl.loop(0, ndev - 1)
        def _(i):
            summary_to(i).wait_send()

    @pl.loop(0, blocks)
    def _(j):
        @pl.when(jnp.logical_not(last & (j == block)))
        def _():
            pltpu.make_async_remote_copy(
                src_ref=own_ref, dst_ref=sum_ref.at[j], send_sem=send_sem.at[0],
                recv_sem=recv_sem.at[j], device_id=(block, member), device_id_type=MESH,
            ).wait_recv()

    next_k.wait()
    next_v.wait()


def fetch(w, keys, values, own, blocks, members):
    ndev = blocks * members
    dma = pltpu.SemaphoreType.DMA
    grid = members == 2 and blocks == 16 and w.shape[0] % 32 == 0
    outs = (
        jax.ShapeDtypeStruct(keys.shape, keys.dtype),
        jax.ShapeDtypeStruct(values.shape, values.dtype),
        jax.ShapeDtypeStruct((blocks,) + own.shape, own.dtype),
    )
    args = (keys, values, own)
    sems = [dma((ndev,)), dma((blocks,)), dma((2,)), dma((2,)), dma]
    if grid:
        outs = (jax.ShapeDtypeStruct((ndev,) + w.shape, w.dtype),) + outs
        args = (w,) + args
        sems += [dma((8,))] + [dma((4,))] * 9 + [dma((2 * blocks,))] * 2 + [dma]
    got = pl.pallas_call(
        functools.partial(fetch_kernel, blocks, members, grid),
        out_shape=outs,
        in_specs=[ANY] * len(args),
        out_specs=(ANY,) * len(outs),
        scratch_shapes=sems,
        compiler_params=pltpu.CompilerParams(has_side_effects=True),
        name="fetch",
    )(*args)
    if grid:
        return (got[0].reshape(ndev * w.shape[0], w.shape[1]),) + tuple(got[1:])
    return (lax.all_gather(w, ("seq", "fsdp"), axis=0, tiled=True),) + tuple(got)


def give_back_kernel(
    blocks, members, ret_ref, gsum_ref, got_ref, parts_ref,
    send_sem, recv_sem, ret_send, ret_recv,
):
    block, member, dev = place()
    ndev = blocks * members
    before = lax.rem(dev + ndev - 1, ndev)
    back = pltpu.make_async_remote_copy(
        src_ref=ret_ref, dst_ref=got_ref, send_sem=ret_send, recv_sem=ret_recv,
        device_id=(before // members, lax.rem(before, members)), device_id_type=MESH,
    )

    def part_to(m):
        return pltpu.make_async_remote_copy(
            src_ref=gsum_ref.at[m], dst_ref=parts_ref.at[dev], send_sem=send_sem.at[m],
            recv_sem=recv_sem.at[dev], device_id=(m, members - 1), device_id_type=MESH,
        )

    back.start()

    @pl.loop(0, blocks)
    def _(m):
        @pl.when(m < block)
        def _():
            part_to(m).start()

    @pl.loop(0, blocks)
    def _(m):
        @pl.when(m < block)
        def _():
            part_to(m).wait_send()

    @pl.when(member == members - 1)
    def _():
        @pl.loop(0, ndev)
        def _(j):
            @pl.when(j >= (block + 1) * members)
            def _():
                pltpu.make_async_remote_copy(
                    src_ref=gsum_ref.at[0], dst_ref=parts_ref.at[j], send_sem=send_sem.at[0],
                    recv_sem=recv_sem.at[j], device_id=(block, member), device_id_type=MESH,
                ).wait_recv()

    back.wait()


def give_back(ret, gsum, blocks, members):
    ndev = blocks * members
    return pl.pallas_call(
        functools.partial(give_back_kernel, blocks, members),
        out_shape=(
            jax.ShapeDtypeStruct(ret.shape, ret.dtype),
            jax.ShapeDtypeStruct((ndev,) + gsum.shape[1:], gsum.dtype),
        ),
        in_specs=[ANY] * 2,
        out_specs=(ANY,) * 2,
        scratch_shapes=[
            pltpu.SemaphoreType.DMA((blocks,)),
            pltpu.SemaphoreType.DMA((ndev,)),
            pltpu.SemaphoreType.DMA,
            pltpu.SemaphoreType.DMA,
        ],
        compiler_params=pltpu.CompilerParams(has_side_effects=True),
        name="give_back",
    )(ret, gsum)


def dot(a, b, da, db):
    return lax.dot_general(a, b, (((da,), (db,)), ((), ())), preferred_element_type=jnp.float32)


def attend_kernel(
    q_ref, k_ref, v_ref, pk_ref, pv_ref, ks_ref, vs_ref, go_ref, w_ref, valid_ref,
    out_ref, gq_ref, gk_ref, gv_ref, ret_ref, gs_ref, total,
):
    f32, b16 = jnp.float32, jnp.bfloat16
    tokens = q_ref.shape[0]
    scale = 1.0 / HEAD_DIM**0.5
    h = pl.program_id(0)
    w = w_ref[...]
    valid = valid_ref[...] > 0
    grads = dot(go_ref[...], w, 1, 1).astype(b16)
    attns = []
    for i in range(HEADS):
        at = slice(i * HEAD_DIM, (i + 1) * HEAD_DIM)
        q, grad = q_ref[:, at], grads[:, at]
        key = jnp.concatenate([pk_ref[:, at], k_ref[:, at], ks_ref[:, at]], axis=0)
        val = jnp.concatenate([pv_ref[:, at], v_ref[:, at], vs_ref[:, at]], axis=0)
        score = jnp.where(valid, dot(q, key, 1, 1) * scale, -jnp.inf)
        top = jnp.max(score, axis=-1, keepdims=True)
        expo = jnp.exp(score - top)
        prob = (expo / jnp.sum(expo, axis=-1, keepdims=True)).astype(b16)
        attns.append(dot(prob, val, 1, 0).astype(b16))
        prob32 = prob.astype(f32)
        gprob = dot(grad, val, 1, 1)
        delta = jnp.sum(prob32 * gprob, axis=-1, keepdims=True)
        gscore = (prob32 * (gprob - delta) * scale).astype(b16)
        gq_ref[:, at] = dot(gscore, key, 1, 0).astype(b16)
        gk = dot(gscore, q, 0, 0)
        gv = dot(prob, grad, 0, 0)
        ret_ref[0, :, at] = gk[:tokens].astype(b16)
        ret_ref[1, :, at] = gv[:tokens].astype(b16)
        gk_ref[:, at] = gk[tokens : 2 * tokens]
        gv_ref[:, at] = gv[tokens : 2 * tokens]
        gs_ref[0, :, at] = gk[2 * tokens :].astype(b16)
        gs_ref[1, :, at] = gv[2 * tokens :].astype(b16)
    part = dot(jnp.concatenate(attns, axis=1), w, 1, 0)

    @pl.when(h == 0)
    def _():
        total[...] = part

    @pl.when(h > 0)
    def _():
        total[...] += part

    @pl.when(h == pl.num_programs(0) - 1)
    def _():
        out_ref[...] = total[...].astype(b16)


def attend(q, k, v, pk, pv, ks, vs, go, w, valid):
    tokens, width = q.shape
    nsum, wide = ks.shape[0], go.shape[1]
    f32, b16 = jnp.float32, jnp.bfloat16
    step = HEADS * HEAD_DIM
    col = pl.BlockSpec((tokens, step), lambda h: (0, h))
    scol = pl.BlockSpec((nsum, step), lambda h: (0, h))
    whole = pl.BlockSpec((tokens, wide), lambda h: (0, 0))
    return pl.pallas_call(
        attend_kernel,
        grid=(width // step,),
        in_specs=[
            col, col, col, col, col, scol, scol, whole,
            pl.BlockSpec((step, wide), lambda h: (h, 0)),
            pl.BlockSpec(valid.shape, lambda h: (0, 0)),
        ],
        out_specs=(
            whole, col, col, col,
            pl.BlockSpec((2, tokens, step), lambda h: (0, 0, h)),
            pl.BlockSpec((2, nsum, step), lambda h: (0, 0, h)),
        ),
        out_shape=(
            jax.ShapeDtypeStruct((tokens, wide), b16),
            jax.ShapeDtypeStruct((tokens, width), b16),
            jax.ShapeDtypeStruct((tokens, width), f32),
            jax.ShapeDtypeStruct((tokens, width), f32),
            jax.ShapeDtypeStruct((2, tokens, width), b16),
            jax.ShapeDtypeStruct((2, nsum, width), b16),
        ),
        scratch_shapes=[pltpu.VMEM((tokens, wide), f32)],
        compiler_params=pltpu.CompilerParams(vmem_limit_bytes=56 * 2**20),
        name="attend",
    )(q, k, v, pk, pv, ks, vs, go, w, valid)


def local(queries, keys, values, grad_out, out_proj, lists, window):
    f32 = jnp.float32
    tokens, width = queries.shape
    blocks, members = lax.axis_size("seq"), lax.axis_size("fsdp")
    ndev = blocks * members
    block, member, dev = place()
    nsum = blocks * SUMMARY
    own = jnp.stack([keys[tokens - SUMMARY :], values[tokens - SUMMARY :]])
    own = own.reshape(16, 2 * SUMMARY * width // 16)
    whole, pk, pv, sums = fetch(out_proj, keys, values, own, blocks, members)
    sums = sums.reshape(blocks, 2, SUMMARY, width)
    ks = sums[:, 0].reshape(nsum, width)
    vs = sums[:, 1].reshape(nsum, width)

    my_list = lax.dynamic_index_in_dim(lists, block, 0, keepdims=False)
    ids = jnp.arange(nsum, dtype=jnp.int32) // SUMMARY
    hit = jnp.any(my_list[:, None] == ids[None, :], axis=0) & (ids < block)
    extent = lax.dynamic_index_in_dim(window, block, 0, keepdims=False)
    rows = jnp.arange(tokens, dtype=jnp.int32)
    cols = jnp.arange(2 * tokens, dtype=jnp.int32)
    offset = rows[:, None] + tokens - cols[None, :]
    near = (offset >= 0) & (offset < extent) & ((cols[None, :] >= tokens) | (dev > 0))
    valid = jnp.concatenate([near, jnp.broadcast_to(hit[None], (tokens, nsum))], axis=1)

    out, gq, gk, gv, ret, gs = attend(
        queries, keys, values, pk, pv, ks, vs, grad_out, whole, valid.astype(f32)
    )
    gs = gs.reshape(2, blocks, SUMMARY, width).transpose(1, 0, 2, 3)
    got, parts = give_back(ret, gs.reshape(blocks, 16, -1), blocks, members)
    got = jnp.where(dev < ndev - 1, got.astype(f32), 0.0)
    sent = (jnp.arange(ndev) >= (block + 1) * members) & (member == members - 1)
    extra = jnp.sum(jnp.where(sent[:, None, None], parts.astype(f32), 0.0), axis=0)
    extra = extra.reshape(2, SUMMARY, width)
    pad = jnp.pad(extra, ((0, 0), (tokens - SUMMARY, 0), (0, 0)))
    grad_keys = (gk + got[0] + pad[0]).astype(jnp.bfloat16)
    grad_values = (gv + got[1] + pad[1]).astype(jnp.bfloat16)
    return out, gq, grad_keys, grad_values


def solution(mesh):
    split = P(("seq", "fsdp"), None)
    return jax.shard_map(
        local, mesh=mesh, in_specs=(split,) * 5 + (P(), P()), out_specs=(split,) * 4, check_vma=False
    )
```

```python
import functools

import jax
import jax.numpy as jnp
from jax import lax
from jax.experimental import pallas as pl
from jax.experimental.pallas import tpu as pltpu
from jax.sharding import PartitionSpec as P

HEAD_DIM = 128
HEADS = 4
SUMMARY = 4
MESH = pl.DeviceIdType.MESH
ANY = pl.BlockSpec(memory_space=pl.ANY)


def place():
    block, member = lax.axis_index("seq"), lax.axis_index("fsdp")
    return block, member, block * lax.axis_size("fsdp") + member


class Grid:
    def __init__(self, w_ref, all_ref, sems):
        self.block, self.member, self.dev = place()
        self.z, self.y, self.x = self.block // 4, lax.rem(self.block // 2, 2), lax.rem(self.block, 2)
        self.w_ref, self.all_ref, self.rows = w_ref, all_ref, w_ref.shape[0] // 2
        (self.z_send, self.z_recv, self.x_send, self.x_recv, self.y_send, self.y_recv, self.dx_send,
         self.dx_recv, self.dy_send, self.dy_recv, self.s_send, self.s_recv, self.l_sem) = sems

    def at(self, z, dy=0, dx=0):
        y = 1 - self.y if dy else self.y
        x = 1 - self.x if dx else self.x
        return z * 4 + y * 2 + x

    def ref(self, block, half=None, other=False):
        shard = block * 2 + (1 - self.member if other else self.member)
        if half is None:
            return self.all_ref.at[shard]
        return self.all_ref.at[shard, pl.ds(half * self.rows, self.rows)]

    def copy(self, ref, to, send, recv):
        return pltpu.make_async_remote_copy(
            src_ref=ref, dst_ref=ref, send_sem=send, recv_sem=recv,
            device_id=(to, self.member), device_id_type=MESH,
        )

    def arrived(self, ref, recv):
        self.copy(ref, self.at(self.z, dx=1), self.x_send.at[0], recv).wait_recv()

    def aside(self, block, half=None, other=False):
        ref = self.ref(block, half, other)
        i = block * 2 + (half or 0)
        return pltpu.make_async_remote_copy(
            src_ref=ref, dst_ref=ref, send_sem=self.s_send.at[i], recv_sem=self.s_recv.at[i],
            device_id=(self.block, 1 - self.member), device_id_type=MESH,
        )

    def up(self, z):
        return self.copy(self.ref(self.at(z)), self.at(self.z + 1), self.z_send.at[z], self.z_recv.at[z])

    def down(self, z):
        return self.copy(self.ref(self.at(z)), self.at(self.z - 1), self.z_send.at[4 + z], self.z_recv.at[z])

    def to_x(self, z):
        return self.copy(self.ref(self.at(z)), self.at(self.z, dx=1), self.x_send.at[z], self.x_recv.at[z])

    def to_y(self, z):
        return self.copy(self.ref(self.at(z)), self.at(self.z, dy=1), self.y_send.at[z], self.y_recv.at[z])

    def on_y(self, z):
        return self.copy(self.ref(self.at(z, dx=1), 0), self.at(self.z, dy=1), self.dy_send.at[z], self.dy_recv.at[z])

    def on_x(self, z):
        return self.copy(self.ref(self.at(z, dy=1), 1), self.at(self.z, dx=1), self.dx_send.at[z], self.dx_recv.at[z])

    def spread(self, z, step):
        if step:
            self.arrived(self.ref(self.at(z)), self.z_recv.at[z])
        if step >= 0:
            @pl.when(self.z > 0)
            def _():
                self.down(z).start()
        if step <= 0:
            @pl.when(self.z < 3)
            def _():
                self.up(z).start()
        self.to_x(z).start()
        self.to_y(z).start()
        self.aside(self.at(z)).start()

    def turn(self, z):
        self.arrived(self.ref(self.at(z, dx=1)), self.x_recv.at[z])
        self.on_y(z).start()
        self.aside(self.at(z, dx=1)).start()
        self.arrived(self.ref(self.at(z, dy=1)), self.y_recv.at[z])
        self.on_x(z).start()
        self.aside(self.at(z, dy=1)).start()

    def corner(self, z):
        self.arrived(self.ref(self.at(z, 1, 1), 0), self.dy_recv.at[z])
        self.aside(self.at(z, 1, 1), 0).start()
        self.arrived(self.ref(self.at(z, 1, 1), 1), self.dx_recv.at[z])
        self.aside(self.at(z, 1, 1), 1).start()

    def each(self, step, do):
        z = self.z + step

        @pl.when((z >= 0) & (z < 4))
        def _():
            do(z)

    def run(self, begin):
        mine = pltpu.make_async_copy(self.w_ref, self.all_ref.at[self.dev], self.l_sem)
        mine.start()
        mine.wait()
        for far in range(4):
            steps = (far, -far) if far else (0,)
            for step in steps:
                self.each(step, functools.partial(self.spread, step=step))
            if far == 0:
                begin()
            for step in steps:
                self.each(step, self.turn)
        for far in range(4):
            for step in (far, -far) if far else (0,):
                self.each(step, self.corner)

        @pl.loop(0, 4)
        def _(z):
            @pl.when((z >= self.z) & (self.z > 0))
            def _():
                self.down(z).wait_send()

            @pl.when((z <= self.z) & (self.z < 3))
            def _():
                self.up(z).wait_send()

            for move in (self.to_x, self.to_y, self.on_x, self.on_y):
                move(z).wait_send()
            for dy, dx, half in ((0, 0, None), (0, 1, None), (1, 0, None), (1, 1, 0), (1, 1, 1)):
                self.aside(self.at(z, dy, dx), half).wait_send()
                self.aside(self.at(z, dy, dx), half, True).wait_recv()


def fetch_kernel(blocks, members, grid, *refs):
    if grid:
        w_ref, refs = refs[0], refs[1:]
        k_ref, v_ref, own_ref, all_ref = refs[:4]
        refs = refs[4:]
    else:
        k_ref, v_ref, own_ref = refs[:3]
        refs = refs[3:]
    pk_ref, pv_ref, sum_ref, send_sem, recv_sem, prev_send, prev_recv, loc_sem = refs[:8]
    block, member, dev = place()
    ndev = blocks * members
    last = member == members - 1

    def to_next(i, src, dst):
        after = lax.rem(dev + 1, ndev)
        return pltpu.make_async_remote_copy(
            src_ref=src, dst_ref=dst, send_sem=prev_send.at[i], recv_sem=prev_recv.at[i],
            device_id=(after // members, lax.rem(after, members)), device_id_type=MESH,
        )

    def summary_to(i):
        to = lax.rem(dev + 1 + i, ndev)
        return pltpu.make_async_remote_copy(
            src_ref=own_ref, dst_ref=sum_ref.at[block], send_sem=send_sem.at[i],
            recv_sem=recv_sem.at[block],
            device_id=(to // members, lax.rem(to, members)), device_id_type=MESH,
        )

    local = pltpu.make_async_copy(own_ref, sum_ref.at[block], loc_sem)

    next_k, next_v = to_next(0, k_ref, pk_ref), to_next(1, v_ref, pv_ref)

    def begin():
        @pl.when(last)
        def _():
            local.start()

            @pl.loop(0, ndev - 1)
            def _(i):
                summary_to(i).start()

        next_k.start()
        next_v.start()

    if grid:
        Grid(w_ref, all_ref, refs[8:]).run(begin)
    else:
        begin()

    @pl.when(last)
    def _():
        local.wait()

        @pl.loop(0, ndev - 1)
        def _(i):
            summary_to(i).wait_send()

    @pl.loop(0, blocks)
    def _(j):
        @pl.when(jnp.logical_not(last & (j == block)))
        def _():
            pltpu.make_async_remote_copy(
                src_ref=own_ref, dst_ref=sum_ref.at[j], send_sem=send_sem.at[0],
                recv_sem=recv_sem.at[j], device_id=(block, member), device_id_type=MESH,
            ).wait_recv()

    next_k.wait()
    next_v.wait()


def fetch(w, keys, values, own, blocks, members):
    ndev = blocks * members
    dma = pltpu.SemaphoreType.DMA
    grid = members == 2 and blocks == 16 and w.shape[0] % 32 == 0
    outs = (
        jax.ShapeDtypeStruct(keys.shape, keys.dtype),
        jax.ShapeDtypeStruct(values.shape, values.dtype),
        jax.ShapeDtypeStruct((blocks,) + own.shape, own.dtype),
    )
    args = (keys, values, own)
    sems = [dma((ndev,)), dma((blocks,)), dma((2,)), dma((2,)), dma]
    if grid:
        outs = (jax.ShapeDtypeStruct((ndev,) + w.shape, w.dtype),) + outs
        args = (w,) + args
        sems += [dma((8,))] + [dma((4,))] * 9 + [dma((2 * blocks,))] * 2 + [dma]
    got = pl.pallas_call(
        functools.partial(fetch_kernel, blocks, members, grid),
        out_shape=outs,
        in_specs=[ANY] * len(args),
        out_specs=(ANY,) * len(outs),
        scratch_shapes=sems,
        compiler_params=pltpu.CompilerParams(has_side_effects=True),
        name="fetch",
    )(*args)
    if grid:
        return (got[0].reshape(ndev * w.shape[0], w.shape[1]),) + tuple(got[1:])
    return (lax.all_gather(w, ("seq", "fsdp"), axis=0, tiled=True),) + tuple(got)


def give_back_kernel(
    blocks, members, ret_ref, gsum_ref, got_ref, parts_ref,
    send_sem, recv_sem, ret_send, ret_recv,
):
    block, member, dev = place()
    ndev = blocks * members
    before = lax.rem(dev + ndev - 1, ndev)
    back = pltpu.make_async_remote_copy(
        src_ref=ret_ref, dst_ref=got_ref, send_sem=ret_send, recv_sem=ret_recv,
        device_id=(before // members, lax.rem(before, members)), device_id_type=MESH,
    )

    def part_to(m):
        return pltpu.make_async_remote_copy(
            src_ref=gsum_ref.at[m], dst_ref=parts_ref.at[dev], send_sem=send_sem.at[m],
            recv_sem=recv_sem.at[dev], device_id=(m, members - 1), device_id_type=MESH,
        )

    @pl.loop(0, blocks)
    def _(m):
        @pl.when(m < block)
        def _():
            part_to(m).start()

    back.start()

    @pl.loop(0, blocks)
    def _(m):
        @pl.when(m < block)
        def _():
            part_to(m).wait_send()

    @pl.when(member == members - 1)
    def _():
        @pl.loop(0, ndev)
        def _(j):
            @pl.when(j >= (block + 1) * members)
            def _():
                pltpu.make_async_remote_copy(
                    src_ref=gsum_ref.at[0], dst_ref=parts_ref.at[j], send_sem=send_sem.at[0],
                    recv_sem=recv_sem.at[j], device_id=(block, member), device_id_type=MESH,
                ).wait_recv()

    back.wait()


def give_back(ret, gsum, blocks, members):
    ndev = blocks * members
    return pl.pallas_call(
        functools.partial(give_back_kernel, blocks, members),
        out_shape=(
            jax.ShapeDtypeStruct(ret.shape, ret.dtype),
            jax.ShapeDtypeStruct((ndev,) + gsum.shape[1:], gsum.dtype),
        ),
        in_specs=[ANY] * 2,
        out_specs=(ANY,) * 2,
        scratch_shapes=[
            pltpu.SemaphoreType.DMA((blocks,)),
            pltpu.SemaphoreType.DMA((ndev,)),
            pltpu.SemaphoreType.DMA,
            pltpu.SemaphoreType.DMA,
        ],
        compiler_params=pltpu.CompilerParams(has_side_effects=True),
        name="give_back",
    )(ret, gsum)


def dot(a, b, da, db):
    return lax.dot_general(a, b, (((da,), (db,)), ((), ())), preferred_element_type=jnp.float32)


def attend_kernel(
    q_ref, k_ref, v_ref, pk_ref, pv_ref, ks_ref, vs_ref, go_ref, w_ref, valid_ref,
    out_ref, gq_ref, gk_ref, gv_ref, ret_ref, gs_ref, total,
):
    f32, b16 = jnp.float32, jnp.bfloat16
    tokens = q_ref.shape[0]
    scale = 1.0 / HEAD_DIM**0.5
    h = pl.program_id(0)
    w = w_ref[...]
    valid = valid_ref[...] > 0
    grads = dot(go_ref[...], w, 1, 1).astype(b16)
    attns = []
    for i in range(HEADS):
        at = slice(i * HEAD_DIM, (i + 1) * HEAD_DIM)
        q, grad = q_ref[:, at], grads[:, at]
        key = jnp.concatenate([pk_ref[:, at], k_ref[:, at], ks_ref[:, at]], axis=0)
        val = jnp.concatenate([pv_ref[:, at], v_ref[:, at], vs_ref[:, at]], axis=0)
        score = jnp.where(valid, dot(q, key, 1, 1) * scale, -jnp.inf)
        top = jnp.max(score, axis=-1, keepdims=True)
        expo = jnp.exp(score - top)
        prob = (expo / jnp.sum(expo, axis=-1, keepdims=True)).astype(b16)
        attns.append(dot(prob, val, 1, 0).astype(b16))
        prob32 = prob.astype(f32)
        gprob = dot(grad, val, 1, 1)
        delta = jnp.sum(prob32 * gprob, axis=-1, keepdims=True)
        gscore = (prob32 * (gprob - delta) * scale).astype(b16)
        gq_ref[:, at] = dot(gscore, key, 1, 0).astype(b16)
        gk = dot(gscore, q, 0, 0)
        gv = dot(prob, grad, 0, 0)
        ret_ref[0, :, at] = gk[:tokens].astype(b16)
        ret_ref[1, :, at] = gv[:tokens].astype(b16)
        gk_ref[:, at] = gk[tokens : 2 * tokens]
        gv_ref[:, at] = gv[tokens : 2 * tokens]
        gs_ref[0, :, at] = gk[2 * tokens :].astype(b16)
        gs_ref[1, :, at] = gv[2 * tokens :].astype(b16)
    part = dot(jnp.concatenate(attns, axis=1), w, 1, 0)

    @pl.when(h == 0)
    def _():
        total[...] = part

    @pl.when(h > 0)
    def _():
        total[...] += part

    @pl.when(h == pl.num_programs(0) - 1)
    def _():
        out_ref[...] = total[...].astype(b16)


def attend(q, k, v, pk, pv, ks, vs, go, w, valid):
    tokens, width = q.shape
    nsum, wide = ks.shape[0], go.shape[1]
    f32, b16 = jnp.float32, jnp.bfloat16
    step = HEADS * HEAD_DIM
    col = pl.BlockSpec((tokens, step), lambda h: (0, h))
    scol = pl.BlockSpec((nsum, step), lambda h: (0, h))
    whole = pl.BlockSpec((tokens, wide), lambda h: (0, 0))
    return pl.pallas_call(
        attend_kernel,
        grid=(width // step,),
        in_specs=[
            col, col, col, col, col, scol, scol, whole,
            pl.BlockSpec((step, wide), lambda h: (h, 0)),
            pl.BlockSpec(valid.shape, lambda h: (0, 0)),
        ],
        out_specs=(
            whole, col, col, col,
            pl.BlockSpec((2, tokens, step), lambda h: (0, 0, h)),
            pl.BlockSpec((2, nsum, step), lambda h: (0, 0, h)),
        ),
        out_shape=(
            jax.ShapeDtypeStruct((tokens, wide), b16),
            jax.ShapeDtypeStruct((tokens, width), b16),
            jax.ShapeDtypeStruct((tokens, width), f32),
            jax.ShapeDtypeStruct((tokens, width), f32),
            jax.ShapeDtypeStruct((2, tokens, width), b16),
            jax.ShapeDtypeStruct((2, nsum, width), b16),
        ),
        scratch_shapes=[pltpu.VMEM((tokens, wide), f32)],
        compiler_params=pltpu.CompilerParams(vmem_limit_bytes=56 * 2**20),
        name="attend",
    )(q, k, v, pk, pv, ks, vs, go, w, valid)


def local(queries, keys, values, grad_out, out_proj, lists, window):
    f32 = jnp.float32
    tokens, width = queries.shape
    blocks, members = lax.axis_size("seq"), lax.axis_size("fsdp")
    ndev = blocks * members
    block, member, dev = place()
    nsum = blocks * SUMMARY
    own = jnp.stack([keys[tokens - SUMMARY :], values[tokens - SUMMARY :]])
    own = own.reshape(16, 2 * SUMMARY * width // 16)
    whole, pk, pv, sums = fetch(out_proj, keys, values, own, blocks, members)
    sums = sums.reshape(blocks, 2, SUMMARY, width)
    ks = sums[:, 0].reshape(nsum, width)
    vs = sums[:, 1].reshape(nsum, width)

    my_list = lax.dynamic_index_in_dim(lists, block, 0, keepdims=False)
    ids = jnp.arange(nsum, dtype=jnp.int32) // SUMMARY
    hit = jnp.any(my_list[:, None] == ids[None, :], axis=0) & (ids < block)
    extent = lax.dynamic_index_in_dim(window, block, 0, keepdims=False)
    rows = jnp.arange(tokens, dtype=jnp.int32)
    cols = jnp.arange(2 * tokens, dtype=jnp.int32)
    offset = rows[:, None] + tokens - cols[None, :]
    near = (offset >= 0) & (offset < extent) & ((cols[None, :] >= tokens) | (dev > 0))
    valid = jnp.concatenate([near, jnp.broadcast_to(hit[None], (tokens, nsum))], axis=1)

    out, gq, gk, gv, ret, gs = attend(
        queries, keys, values, pk, pv, ks, vs, grad_out, whole, valid.astype(f32)
    )
    gs = gs.reshape(2, blocks, SUMMARY, width).transpose(1, 0, 2, 3)
    got, parts = give_back(ret, gs.reshape(blocks, 16, -1), blocks, members)
    got = jnp.where(dev < ndev - 1, got.astype(f32), 0.0)
    sent = (jnp.arange(ndev) >= (block + 1) * members) & (member == members - 1)
    extra = jnp.sum(jnp.where(sent[:, None, None], parts.astype(f32), 0.0), axis=0)
    extra = extra.reshape(2, SUMMARY, width)
    pad = jnp.pad(extra, ((0, 0), (tokens - SUMMARY, 0), (0, 0)))
    grad_keys = (gk + got[0] + pad[0]).astype(jnp.bfloat16)
    grad_values = (gv + got[1] + pad[1]).astype(jnp.bfloat16)
    return out, gq, grad_keys, grad_values


def solution(mesh):
    split = P(("seq", "fsdp"), None)
    return jax.shard_map(
        local, mesh=mesh, in_specs=(split,) * 5 + (P(), P()), out_specs=(split,) * 4, check_vma=False
    )
```
